128 devices in a mesh: gr: 8 (over z_hi, y), gc: 16 (over z_lo, x, core).
Axes of the slice: x: 4, y: 4, z: 4 (z_hi: 2, z_lo: 2; z = z_hi * 2 + z_lo), core: 2. Of those that a mesh axis runs over, the one named last changes fastest.
Arguments:
- a_matrix: bfloat16 [65536, 18432], P('gr', 'gc'), may hold values from -0.5 to 0.5
- scaling: float32 [18432], P('gc'), may hold values from 0.1 to 1
Outputs:
- normal_slab: float32 [1024, 65536], P('gc', 'gr')
The draws below stay inside these ranges and needn't reach their ends.
All inputs are finite; a program needn't handle non-finite values.
Results may differ from the reference program's by a relative error of at most 0.0027.
Values may be sent and summed in bfloat16 or wider, within the bound.
No kernel may reach another device: no remote copies, remote signals or barrier semaphores. Data moves between devices by JAX's collectives and lax.ppermute only.
A program may use at most 128 MiB of HBM per device.

```python
import math
import jax
import jax.numpy as jnp
from jax import lax

M = 65536
SLAB_DEV = 128
K = 18432
N_GR = 8


def block_scale(key, shape, split, least, top_value):
    def one(dim, shards_of):
        draws = jax.random.uniform(jax.random.fold_in(jax.random.fold_in(key, 6), dim), (shards_of,), jnp.float32, least / len(split), top_value / len(split))
        return jnp.repeat(jnp.exp(draws), shape[dim] // shards_of).reshape((-1,) + (1,) * (len(shape) - dim - 1))

    loudness = one(*split[0])
    for cut in split[1:]:
        loudness = loudness * one(*cut)
    return loudness


def centred(rng, extent, deviation, reach, cuts=(), dtype=jnp.bfloat16):
    array = deviation * jax.random.normal(rng, extent, jnp.float32)
    if cuts:
        array = array * block_scale(rng, extent, cuts, -0.22, 0.18)
    return jnp.clip(array, -reach, reach).astype(dtype)


def setup_inputs(seed: int = 0) -> dict:
    arg_keys = jax.random.split(jax.random.key(seed), 3)
    a_matrix = centred(arg_keys[0], (M, K), 128 ** -0.5, 0.5, ((0, 8), (1, 16)))
    scaling = jnp.clip(jnp.exp(math.log(1.0) - 2.3025851 * jax.random.uniform(arg_keys[1], (K,), jnp.float32) ** block_scale(arg_keys[1], (K,), ((0, 16),), -0.2, 0.2)), 0.1, 1.0)
    return {"a_matrix": a_matrix, "scaling": scaling}


def reference(a_matrix, scaling):
    blocks = a_matrix.reshape(N_GR, M // N_GR, K)
    slab = blocks[:, :SLAB_DEV, :].reshape(SLAB_DEV * N_GR, K)
    scaled = (slab.astype(jnp.float32) * scaling[None, :]).astype(jnp.bfloat16)
    left = scaled.astype(jnp.float32)

    def one_block(rows):
        return lax.dot_general(left, rows.astype(jnp.float32), (((1,), (1,)), ((), ())), precision=lax.Precision.HIGHEST, preferred_element_type=jnp.float32)

    parts = lax.map(one_block, blocks)
    return jnp.transpose(parts, (1, 0, 2)).reshape(SLAB_DEV * N_GR, M)
```

```python
import jax
import jax.numpy as jnp
from jax import lax
from jax.experimental import pallas as pl
from jax.experimental.pallas import tpu as pltpu
from jax.sharding import PartitionSpec as P

F32, BF16 = jnp.float32, jnp.bfloat16
SLAB_DEV = 128
HALF = 64
VMEM = 47 * 1024 * 1024

Y_UP = [(z * 4 + y, z * 4 + (y + 1) % 4) for z in range(2) for y in range(4)]
Y_DOWN = [(d, s) for s, d in Y_UP]
Y_FAR = [(z * 4 + y, z * 4 + (y + 2) % 4) for z in range(2) for y in range(4)]
Z_FAR = [(z * 4 + y, (1 - z) * 4 + y) for z in range(2) for y in range(4)]


def gc(z, x, c):
    return (z * 4 + x % 4) * 2 + c


EACH = [(z, x, c) for z in range(2) for x in range(4) for c in range(2)]
X_UP = [(gc(z, x, c), gc(z, x + 1, c)) for z, x, c in EACH]
X_DOWN = [(gc(z, x, c), gc(z, x - 1, c)) for z, x, c in EACH]
Z_NEAR = [(gc(z, x, c), gc(1 - z, x, c)) for z, x, c in EACH]
CORE = [(gc(z, x, c), gc(z, x, 1 - c)) for z, x, c in EACH]

UNITS = [[256, 256, 512], [512, 256, 256]]
PLAN = [
    ("order", 0, 0),
    ("product", 0, 0),
    ("product", 0, 1),
    ("first", 0, 0),
    ("product", 0, 2),
    ("first", 0, 1),
    ("second", 0, 0),
    ("order", 1, 0),
    ("first", 0, 2),
    ("product", 1, 0),
    ("second", 0, 1),
    ("sum", 0, 0),
    ("first", 1, 0),
    ("product", 1, 1),
    ("second", 0, 2),
    ("sum", 0, 1),
    ("product", 1, 2),
    ("first", 1, 1),
    ("second", 1, 0),
    ("sum", 0, 2),
    ("first", 1, 2),
    ("second", 1, 1),
    ("sum", 1, 0),
    ("second", 1, 2),
    ("sum", 1, 1),
    ("finish", 1, 0),
    ("finish", 1, 1),
    ("sum", 1, 2),
    ("finish", 1, 2),
]


def dot(s, a):
    return lax.dot_general(s, a, (((1,), (1,)), ((), ())), preferred_element_type=F32)


def cost(flops, nbytes):
    return pl.CostEstimate(flops=flops, bytes_accessed=nbytes, transcendentals=0)


def params():
    return pltpu.CompilerParams(vmem_limit_bytes=VMEM)


def order_one(place, *refs):
    pieces, out = refs[:4], refs[4]
    for d in range(4):
        for h in range(2):
            to = (place[1] ^ h) * 4 + (d + place[0]) % 4
            out[pl.ds(pl.multiple_of(to * HALF, HALF), HALF), :] = pieces[d][h * HALF : (h + 1) * HALF, :]


def order(place, pieces, dep):
    k = pieces[0].shape[1]
    whole = lambda: (0, 0)
    ins = [(place, None, pltpu.SMEM)] + [(piece, piece.shape, whole) for piece in pieces]
    return run(order_one, (), [(((4 * SLAB_DEV, k), BF16), (4 * SLAB_DEV, k), whole)], ins, dep)[0]


def run(kernel, grid, outs, ins, dep, aliases={}):
    shapes = [jax.ShapeDtypeStruct(shape, dtype) for (shape, dtype), _, _ in outs]
    out_specs = [pl.BlockSpec(block, where) for _, block, where in outs]
    in_specs = [pl.BlockSpec(block, where) if block else pl.BlockSpec(memory_space=where) for _, block, where in ins]
    arrays = [array for array, _, _ in ins]
    arrays += dep
    in_specs += [pl.BlockSpec(memory_space=pl.ANY)] * len(dep)

    def body(*refs):
        kernel(*refs[: len(ins)], *refs[len(arrays) :])

    return pl.pallas_call(
        body,
        grid=grid,
        out_shape=shapes,
        in_specs=in_specs,
        out_specs=out_specs,
        input_output_aliases=aliases,
        compiler_params=params(),
        cost_estimate=cost(1000, 1000),
    )(*arrays)


def product(slab, a, start, n, tile, dep):
    rows, k = slab.shape[0] // 2, slab.shape[1]

    def kernel(s, a_ref, own, sibling):
        total = dot(s[...], a_ref[...])
        own[...] = total[:rows]
        sibling[...] = total[rows:].astype(BF16)

    return run(
        kernel,
        (n // tile,),
        [(((rows, n), F32), (rows, tile), lambda i: (0, i)), (((rows, n), BF16), (rows, tile), lambda i: (0, i))],
        [(slab, (2 * rows, k), lambda i: (0, 0)), (a, (tile, k), lambda i: (start // tile + i, 0))],
        dep,
    )


def first_messages(own, came, tile, dep):
    half = own.shape[1] // 2
    tile = min(half, tile)
    to = half // tile

    def kernel(l, r, c_l, c_r, up, down):
        up[:HALF] = (l[128:192] + wide(c_l[128:192])).astype(BF16)
        up[HALF:] = (r[64:128] + wide(c_r[64:128])).astype(BF16)
        down[:HALF] = (r[128:192] + wide(c_r[128:192])).astype(BF16)
        down[HALF:] = (l[192:256] + wide(c_l[192:256])).astype(BF16)

    left, right = lambda i: (0, i), lambda i: (0, to + i)
    return run(
        kernel,
        (to,),
        [(((128, half), BF16), (128, tile), left)] * 2,
        [(own, (256, tile), left), (own, (256, tile), right), (came, (256, tile), left), (came, (256, tile), right)],
        dep,
    )


def second_messages(own, came, up1, down1, tile, dep):
    half = own.shape[1] // 2
    tile = min(half, tile)
    to = half // tile

    def kernel(o1, c1, u, o3, c3, d, up, down):
        up[...] = (o1[...] + wide(c1[...]) + wide(u[...])).astype(BF16)
        down[...] = (o3[...] + wide(c3[...]) + wide(d[...])).astype(BF16)

    block = (64, tile)
    first = lambda i: (0, i)
    return run(
        kernel,
        (to,),
        [(((64, half), BF16), block, first)] * 2,
        [
            (own, block, lambda i: (1, i)),
            (came, block, lambda i: (1, i)),
            (up1, block, first),
            (own, block, lambda i: (3, to + i)),
            (came, block, lambda i: (3, to + i)),
            (down1, block, first),
        ],
        dep,
    )


def x_parts(own, came, up1, down1, up2, down2, tile):
    half = own.shape[1] // 2
    to = half // tile
    block = (64, tile)
    cut = lambda j, i: (0, j * to + i)
    low = lambda j, i: (0, i)
    high = lambda j, i: (1, i)
    ins = [(own, block, cut), (came, block, cut)]
    ins += [(up2, block, low), (down1, block, high), (down2, block, low), (up1, block, high)]
    return (2, to), cut, ins


def x_total(o, c, u2, d1, d2, u1):
    left = pl.program_id(0) == 0
    return o[...] + wide(c[...]) + jnp.where(left, wide(u2[...]) + wide(d1[...]), wide(d2[...]) + wide(u1[...]))


def sum_over_x(parts, held, start, tile, dep):
    n = parts[0].shape[1]
    tile = min(n // 2, tile)
    grid, cut, ins = x_parts(*parts, tile)
    at = start // tile
    spread = lambda j, i: (0, at + cut(j, i)[1])

    def kernel(o, c, u2, d1, d2, u1, _, out):
        out[...] = x_total(o, c, u2, d1, d2, u1)

    return run(
        kernel,
        grid,
        [((held.shape, F32), (64, tile), spread)],
        ins + [(held, None, pl.ANY)],
        dep,
        {6: 0},
    )[0]


def split_over_z(parts, held, start, same, tile, dep):
    n = parts[0].shape[1]
    tile = min(n // 2, tile)
    grid, cut, ins = x_parts(*parts, tile)
    at = start // tile
    spread = lambda j, i: (0, at + cut(j, i)[1])

    def kernel(o, c, u2, d1, d2, u1, h, same_ref, stays, goes):
        total = x_total(o, c, u2, d1, d2, u1)
        yes = same_ref[0] == 1
        stays[...] = jnp.where(yes, h[...], total)
        goes[...] = jnp.where(yes, total, h[...]).astype(BF16)

    return run(
        kernel,
        grid,
        [(((64, n), F32), (64, tile), cut), (((64, n), BF16), (64, tile), cut)],
        ins + [(held, (64, tile), spread), (same, None, pltpu.SMEM)],
        dep,
    )


def finish(stays, came, out, start, tile, dep):
    n = stays.shape[1]
    tile = min(n, tile)
    at = start // tile

    def kernel(s, c, _, o):
        o[...] = s[...] + wide(c[...])

    here = lambda i: (0, i)
    return run(
        kernel,
        (n // tile,),
        [((out.shape, F32), (64, tile), lambda i: (0, at + i))],
        [(stays, (64, tile), here), (came, (64, tile), here), (out, None, pl.ANY)],
        dep,
        {2: 0},
    )[0]


def wide(v):
    return v.astype(F32)


def shards(a, scaling):
    n_all = a.shape[0]
    gr, at = lax.axis_index("gr"), lax.axis_index("gc")
    core, x, z_lo = at % 2, (at // 2) % 4, at // 8
    y, z_hi = gr % 4, gr // 4
    same = (z_lo == z_hi)
    place = jnp.stack([(y - x + 4) % 4, core, z_lo ^ z_hi]).astype(jnp.int32)

    mine = (a[:SLAB_DEV].astype(F32) * scaling[None, :]).astype(BF16)
    y_up = lax.ppermute(mine, "gr", Y_UP)
    y_down = lax.ppermute(mine, "gr", Y_DOWN)
    y_far = lax.ppermute(mine, "gr", Y_FAR)
    z_far = lax.ppermute(mine, "gr", Z_FAR)
    near = [mine, y_down, y_far, y_up]
    far = [z_far, lax.ppermute(z_far, "gr", Y_DOWN), lax.ppermute(y_far, "gr", Z_FAR), lax.ppermute(z_far, "gr", Y_UP)]
    slabs = [None, None]
    tile = n_all // 8
    start = [[0], [0]]
    for e in range(2):
        for size in UNITS[e]:
            start[e].append(start[e][-1] + size * n_all // 1024)
    held = jnp.zeros((HALF, n_all), F32)
    out = jnp.zeros((HALF, n_all), F32)
    flag = same.astype(jnp.int32).reshape(1)
    units, z_units = {}, {}
    dep = [z_far]
    for what, e, i in PLAN:
        if what == "order":
            slabs[e] = order(place, far if e else near, dep)
            dep = [slabs[e]]
            continue
        begin, n = start[e][i], start[e][i + 1] - start[e][i]
        if what == "product":
            own, sibling = product(slabs[e], a, begin, n, tile, dep)
            units[e, i] = [own, lax.ppermute(sibling, "gc", CORE)]
            dep = [sibling]
        elif what == "first":
            if e == i == 0:
                dep += far
            up, down = first_messages(*units[e, i], tile, dep)
            units[e, i] += [lax.ppermute(up, "gc", X_UP), lax.ppermute(down, "gc", X_DOWN)]
            dep = [down]
        elif what == "second":
            up, down = second_messages(*units[e, i], tile, dep)
            units[e, i] += [lax.ppermute(up, "gc", X_UP), lax.ppermute(down, "gc", X_DOWN)]
            dep = [down]
        elif what == "sum" and e == 0:
            held = sum_over_x(units[e, i], held, begin, tile, dep)
            dep = [held]
        elif what == "sum":
            stays, goes = split_over_z(units[e, i], held, begin, flag, tile, dep)
            z_units[i] = stays, lax.ppermute(goes, "gc", Z_NEAR)
            dep = [goes]
        else:
            out = finish(*z_units[i], out, begin, tile, dep)
            dep = [out]
    return out


def solution(mesh):
    placed = (P("gr", "gc"), P("gc"))
    return jax.shard_map(shards, mesh=mesh, in_specs=placed, out_specs=P("gc", "gr"), check_vma=False)
```

```python
import jax
import jax.numpy as jnp
from jax import lax
from jax.experimental import pallas as pl
from jax.experimental.pallas import tpu as pltpu
from jax.sharding import PartitionSpec as P

F32, BF16 = jnp.float32, jnp.bfloat16
SLAB_DEV = 128
LONG = 100_000_000
HALF = 64
CHIP = 128
VMEM = 20 * 1024 * 1024

Y_UP = [(z * 4 + y, z * 4 + (y + 1) % 4) for z in range(2) for y in range(4)]
Y_DOWN = [(d, s) for s, d in Y_UP]
Y_FAR = [(z * 4 + y, z * 4 + (y + 2) % 4) for z in range(2) for y in range(4)]
Z_FAR = [(z * 4 + y, (1 - z) * 4 + y) for z in range(2) for y in range(4)]


def gc(z, x, c):
    return (z * 4 + x % 4) * 2 + c


EACH = [(z, x, c) for z in range(2) for x in range(4) for c in range(2)]
X_UP = [(gc(z, x, c), gc(z, x + 1, c)) for z, x, c in EACH]
X_DOWN = [(gc(z, x, c), gc(z, x - 1, c)) for z, x, c in EACH]
Z_NEAR = [(gc(z, x, c), gc(1 - z, x, c)) for z, x, c in EACH]
CORE = [(gc(z, x, c), gc(z, x, 1 - c)) for z, x, c in EACH]

UNITS = [256, 512, 256]
PLAN = [
    ("cut", 0),
    ("cut", 1),
    ("cut", 2),
    ("order", 0),
    ("product", (0, 0)),
    ("send", (0, 0), None),
    ("product", (0, 1)),
    ("send", (0, 1), (0, 0)),
    ("order", 1),
    ("product", (1, 1)),
    ("product", (2, 2)),
    ("send", (1, 1), (0, 1)),
    ("product", (1, 0)),
    ("sum", (0, 0)),
    ("send", (1, 0), (1, 1)),
    ("sum", (0, 1)),
    ("send", (2, 2), (1, 0)),
    ("sum", (1, 1)),
    ("sum", (1, 0)),
    ("send", None, (2, 2)),
    ("swap", (1, 1)),
    ("sum", (2, 2)),
    ("swap", (1, 0)),
]


def dot(s, a):
    return lax.dot_general(s, a, (((1,), (1,)), ((), ())), preferred_element_type=F32)


def cost(flops, nbytes):
    return pl.CostEstimate(flops=flops, bytes_accessed=nbytes, transcendentals=0)


def params():
    return pltpu.CompilerParams(vmem_limit_bytes=VMEM)


def run(kernel, grid, outs, ins, dep, nbytes=1000):
    shapes = [jax.ShapeDtypeStruct(shape, dtype) for (shape, dtype), _, _ in outs]
    spec = lambda block, where: pl.BlockSpec(block, where) if block else pl.BlockSpec(memory_space=where)
    out_specs = [spec(block, where) for _, block, where in outs]
    in_specs = [spec(block, where) for _, block, where in ins]
    arrays = [array for array, _, _ in ins]
    arrays += dep
    in_specs += [pl.BlockSpec(memory_space=pl.ANY)] * len(dep)

    def body(*refs):
        kernel(*refs[: len(ins)], *refs[len(arrays) :])

    return pl.pallas_call(
        body,
        grid=grid,
        out_shape=shapes,
        in_specs=in_specs,
        out_specs=out_specs,
        compiler_params=params(),
        cost_estimate=cost(1000, nbytes),
    )(*arrays)


def vmem(arrays):
    return [(array, None, pltpu.VMEM) for array in arrays]


def over(n, step, body):
    step = min(n, step)

    def one(i, carry):
        body(pl.multiple_of(i * step, step), step)
        return carry

    lax.fori_loop(0, n // step, one, 0)


def cut(a, place, start, n, tile, dep):
    k, half = a.shape[1], a.shape[0] // 2

    def kernel(at, a_ref, *refs):
        refs[-1][...] = a_ref[...]

    return pl.pallas_call(
        kernel,
        grid_spec=pltpu.PrefetchScalarGridSpec(
            num_scalar_prefetch=1,
            grid=(n // tile,),
            in_specs=[pl.BlockSpec((tile, k), lambda i, at: ((1 - at[1]) * (half // tile) + start // tile + i, 0))]
            + [pl.BlockSpec(memory_space=pl.ANY)] * len(dep),
            out_specs=pl.BlockSpec((tile, k), lambda i, at: (i, 0)),
        ),
        out_shape=jax.ShapeDtypeStruct((n, k), BF16),
        compiler_params=params(),
        cost_estimate=cost(1000, 1000),
    )(place, a, *dep)


def order(place, pieces, dep):
    k = pieces[0].shape[1]

    def kernel(at, *refs):
        for d in range(4):
            to = (d + at[0]) % 4
            refs[4][pl.ds(pl.multiple_of(to * CHIP, CHIP), CHIP), :] = refs[d][...]

    ins = [(place, None, pltpu.SMEM)] + vmem(pieces)
    return run(kernel, (), [(((4 * CHIP, k), BF16), None, pltpu.VMEM)], ins, dep)[0]


def product(slabs, a, other, place, start, tile, dep):
    n, k = other.shape
    half = a.shape[0] // 2
    halves = len(slabs) // 2
    rows = slabs[0].shape[0]

    def kernel(at, *refs):
        s, (a_ref, o_ref), outs = refs[: 2 * halves], refs[2 * halves : 2 * halves + 2], refs[-halves:]
        for kind in range(halves):
            if halves == 1:
                mine, theirs = s[0][...], s[1][...]
            else:
                first = at[2] == kind
                mine, theirs = jnp.where(first, s[0][...], s[2][...]), jnp.where(first, s[1][...], s[3][...])
            total = dot(mine, a_ref[...]) + dot(theirs, o_ref[...])
            outs[kind][...] = total.astype(outs[kind].dtype)

    block = pl.BlockSpec((rows, tile), lambda i, at: (0, i))
    return pl.pallas_call(
        kernel,
        grid_spec=pltpu.PrefetchScalarGridSpec(
            num_scalar_prefetch=1,
            grid=(n // tile,),
            in_specs=[pl.BlockSpec((rows, k), lambda i, at: (0, 0))] * (2 * halves)
            + [
                pl.BlockSpec((tile, k), lambda i, at: (at[1] * (half // tile) + start // tile + i, 0)),
                pl.BlockSpec((tile, k), lambda i, at: (i, 0)),
            ]
            + [pl.BlockSpec(memory_space=pl.ANY)] * len(dep),
            out_specs=[block] * halves,
        ),
        out_shape=[jax.ShapeDtypeStruct((rows, n), dtype) for dtype in (F32, BF16)[:halves]],
        compiler_params=params(),
        cost_estimate=cost(1000, LONG),
    )(place, *slabs, a, other, *dep)


def added(refs, block, columns):
    total = None
    for ref in refs:
        term = wide(ref[block * CHIP : (block + 1) * CHIP, columns])
        total = term if total is None else total + term
    return total


class Unit:
    def __init__(self, terms, n):
        self.terms, self.n, self.half = terms, n, n // 2


def send(first, second, dep):
    n_first = first.half if first else 0
    n_second = second.half // 2 if second else 0
    ins = first.terms if first else []
    ins2 = second.terms + [second.up1, second.down1] if second else []

    def kernel(*refs):
        terms, terms2 = refs[: len(ins)], refs[len(ins) : len(ins) + len(ins2) - 2]
        up, down = refs[-2:]

        def one(c, step):
            left, right = pl.ds(c, step), pl.ds(n_first + c, step)
            up[:CHIP, left] = added(terms, 2, left).astype(BF16)
            up[CHIP:, left] = added(terms, 1, right).astype(BF16)
            down[:CHIP, left] = added(terms, 2, right).astype(BF16)
            down[CHIP:, left] = added(terms, 3, left).astype(BF16)

        def two(c, step):
            up1, down1 = refs[len(ins) + len(ins2) - 2 : len(ins) + len(ins2)]
            to = pl.ds(n_first + c, step)
            for i in range(2):
                rows = slice(i * CHIP, (i + 1) * CHIP)
                here = pl.ds(i * n_second + c, step)
                there = pl.ds((i + 2) * n_second + c, step)
                up[rows, to] = (added(terms2, 1, here) + wide(up1[:CHIP, here])).astype(BF16)
                down[rows, to] = (added(terms2, 3, there) + wide(down1[:CHIP, here])).astype(BF16)

        if first:
            over(n_first, 128, one)
        if second:
            over(n_second, 128, two)

    shape = (2 * CHIP, n_first + n_second), BF16
    up, down = run(kernel, (), [(shape, None, pltpu.VMEM)] * 2, vmem(ins + ins2), dep, LONG)
    up, down, dep = lax.ppermute(up, "gc", X_UP), lax.ppermute(down, "gc", X_DOWN), [down]
    if first:
        first.up1, first.down1 = up, down
    if second:
        second.up2, second.down2, second.at = up, down, n_first
    return dep


def sum_over_x(unit, outs, extra, store, dep):
    n_terms, half, at = len(unit.terms), unit.half, unit.at

    def kernel(*refs):
        terms = refs[:n_terms]
        up1, down1, up2, down2 = refs[n_terms : n_terms + 4]
        rest = refs[n_terms + 4 :]

        def one(c, step):
            for i in range(2):
                low, rows = i * (half // 2), slice(i * CHIP, (i + 1) * CHIP)
                here, moved = pl.ds(low + c, step), pl.ds(at + c, step)
                left = added(terms, 0, here) + wide(up2[rows, moved]) + wide(down1[CHIP:, here])
                store(low + c, step, left, rest)
                right = added(terms, 0, pl.ds(half + low + c, step)) + wide(down2[rows, moved]) + wide(up1[CHIP:, here])
                store(half + low + c, step, right, rest)

        over(half // 2, 128, one)

    ins = vmem(unit.terms + [unit.up1, unit.down1, unit.up2, unit.down2]) + extra
    return run(kernel, (), outs, ins, dep, LONG)


def keep(unit, dep):
    def store(c, step, total, refs):
        refs[0][:, pl.ds(c, step)] = total

    return sum_over_x(unit, [(((CHIP, unit.n), F32), None, pltpu.VMEM)], [], store, dep)[0]


def split_over_z(unit, held, place, dep):
    def store(c, step, total, refs):
        h, at, stays, goes = refs
        to = pl.ds(c, step)
        yes = at[2] == 0
        stays[:, to] = jnp.where(yes, h[:, to], total)
        goes[:, to] = jnp.where(yes, total, h[:, to]).astype(BF16)

    shape = CHIP, unit.n
    outs = [((shape, F32), None, pltpu.VMEM), ((shape, BF16), None, pltpu.VMEM)]
    return sum_over_x(unit, outs, vmem([held]) + [(place, None, pltpu.SMEM)], store, dep)


def split_rows(place, at, total):
    first = place[1] == 0
    top, low = total[:HALF], total[HALF:]
    return jnp.where(first, top, low), jnp.where(first, low, top)


def swap(stays, came, place, dep):
    n = stays.shape[1]

    def kernel(s, c, at, mine, theirs):
        def one(c0, step):
            to = pl.ds(c0, step)
            mine[:, to], theirs[:, to] = split_rows(at, None, s[:, to] + wide(c[:, to]))

        over(n, 128, one)

    shape = (HALF, n), F32
    return run(kernel, (), [(shape, None, pltpu.VMEM)] * 2, vmem([stays, came]) + [(place, None, pltpu.SMEM)], dep)


def keep_rows(unit, place, dep):
    def store(c, step, total, refs):
        at, mine, theirs = refs
        mine[:, pl.ds(c, step)], theirs[:, pl.ds(c, step)] = split_rows(at, None, total)

    outs = [(((HALF, unit.n), F32), None, pltpu.VMEM)] * 2
    return sum_over_x(unit, outs, [(place, None, pltpu.SMEM)], store, dep)


def wide(v):
    return v.astype(F32)


def shards(a, scaling):
    n_half = a.shape[0] // 2
    gr, at = lax.axis_index("gr"), lax.axis_index("gc")
    core, x, z_lo = at % 2, (at // 2) % 4, at // 8
    y, z_hi = gr % 4, gr // 4
    place = jnp.stack([(y - x + 4) % 4, core, z_lo ^ z_hi]).astype(jnp.int32)
    tile = n_half // 4
    start = [0]
    for size in UNITS:
        start.append(start[-1] + size * n_half // 1024)

    mine = (a[:SLAB_DEV].astype(F32) * scaling[None, :]).astype(BF16)
    y_up = lax.ppermute(mine, "gr", Y_UP)
    y_down = lax.ppermute(mine, "gr", Y_DOWN)
    y_far = lax.ppermute(mine, "gr", Y_FAR)
    z_far = lax.ppermute(mine, "gr", Z_FAR)
    near = [mine, y_down, y_far, y_up]
    far = [z_far, lax.ppermute(z_far, "gr", Y_DOWN), lax.ppermute(y_far, "gr", Z_FAR), lax.ppermute(z_far, "gr", Y_UP)]

    a = pltpu.with_memory_space_constraint(a, pltpu.HBM)
    dep = [y_up]
    others, parts = {}, {}

    slabs, units, held, z_parts, done = {}, {}, {}, {}, {}
    for what, *names in PLAN:
        name = names[0]
        if what == "cut":
            part = cut(a, place, start[name], start[name + 1] - start[name], tile, dep)
            parts[name] = part
            dep = [part]
        elif what == "order":
            dep = dep + [z_far]
            own = order(place, far if name else near, dep)
            slabs[name] = [own, lax.ppermute(own, "gc", CORE)]
            if name == 0:
                for i in range(len(UNITS)):
                    start_after = (y_down, y_far, z_far) if i == 0 else (slabs[0][1], others[0])
                    part = lax.optimization_barrier((parts[i], *start_after))[0]
                    others[i] = lax.ppermute(part, "gc", CORE)
            dep = [own]
        elif what == "product":
            e, i = name
            if name == (0, 1):
                dep = dep + far
            operands = slabs[0] + slabs[1] if e == 2 else slabs[e]
            own, *sent = product(operands, a, others[i], place, start[i], tile, dep)
            units[name] = Unit([own] + [lax.ppermute(v, "gc", Z_NEAR) for v in sent], others[i].shape[0])
            dep = [own]
        elif what == "send":
            dep = send(*(units[name] if name else None for name in names), dep)
        elif what == "sum" and name[0] == 0:
            held[name[1]] = keep(units[name], dep)
            dep = [held[name[1]]]
        elif what == "sum" and name[0] == 1:
            stays, goes = split_over_z(units[name], held[name[1]], place, dep)
            z_parts[name[1]] = stays, lax.ppermute(goes, "gc", Z_NEAR)
            dep = [goes]
        else:
            if what == "swap":
                own, given = swap(*z_parts[name[1]], place, dep)
            else:
                own, given = keep_rows(units[name], place, dep)
            done[name[1]] = own, lax.ppermute(given, "gc", CORE)
            dep = [given]
    own, came = (jnp.concatenate([done[i][j] for i in range(len(UNITS))], axis=1) for j in range(2))
    first = core == 0
    return jnp.concatenate([jnp.where(first, own, came), jnp.where(first, came, own)], axis=1)


def solution(mesh):
    placed = (P("gr", "gc"), P("gc"))
    return jax.shard_map(shards, mesh=mesh, in_specs=placed, out_specs=P("gc", "gr"), check_vma=False)
```

```python
import jax
import jax.numpy as jnp
from jax import lax
from jax.experimental import pallas as pl
from jax.experimental.pallas import tpu as pltpu
from jax.sharding import PartitionSpec as P

F32, BF16 = jnp.float32, jnp.bfloat16
SLAB_DEV = 128
LONG = 100_000_000
HALF = 64
CHIP = 128
VMEM = 20 * 1024 * 1024

Y_UP = [(z * 4 + y, z * 4 + (y + 1) % 4) for z in range(2) for y in range(4)]
Y_DOWN = [(d, s) for s, d in Y_UP]
Y_FAR = [(z * 4 + y, z * 4 + (y + 2) % 4) for z in range(2) for y in range(4)]
Z_FAR = [(z * 4 + y, (1 - z) * 4 + y) for z in range(2) for y in range(4)]


def gc(z, x, c):
    return (z * 4 + x % 4) * 2 + c


EACH = [(z, x, c) for z in range(2) for x in range(4) for c in range(2)]
X_UP = [(gc(z, x, c), gc(z, x + 1, c)) for z, x, c in EACH]
X_DOWN = [(gc(z, x, c), gc(z, x - 1, c)) for z, x, c in EACH]
Z_NEAR = [(gc(z, x, c), gc(1 - z, x, c)) for z, x, c in EACH]
CORE = [(gc(z, x, c), gc(z, x, 1 - c)) for z, x, c in EACH]

UNITS = [256, 512, 256]
PLAN = [
    ("cut", 0),
    ("cut", 1),
    ("cut", 2),
    ("order", 0),
    ("product", (0, 0)),
    ("send", (0, 0), None),
    ("product", (0, 1)),
    ("send", (0, 1), (0, 0)),
    ("order", 1),
    ("product", (1, 1)),
    ("send", (1, 1), (0, 1)),
    ("product", (2, 2)),
    ("product", (1, 0)),
    ("sum", (0, 0)),
    ("send", (1, 0), (1, 1)),
    ("sum", (0, 1)),
    ("sum", (1, 1)),
    ("send", (2, 2), (1, 0)),
    ("sum", (1, 0)),
    ("send", None, (2, 2)),
    ("swap", (1, 1)),
    ("sum", (2, 2)),
    ("swap", (1, 0)),
]


def dot(s, a):
    return lax.dot_general(s, a, (((1,), (1,)), ((), ())), preferred_element_type=F32)


def cost(flops, nbytes):
    return pl.CostEstimate(flops=flops, bytes_accessed=nbytes, transcendentals=0)


def params():
    return pltpu.CompilerParams(vmem_limit_bytes=VMEM)


def run(kernel, grid, outs, ins, dep, nbytes=1000):
    shapes = [jax.ShapeDtypeStruct(shape, dtype) for (shape, dtype), _, _ in outs]
    spec = lambda block, where: pl.BlockSpec(block, where) if block else pl.BlockSpec(memory_space=where)
    out_specs = [spec(block, where) for _, block, where in outs]
    in_specs = [spec(block, where) for _, block, where in ins]
    arrays = [array for array, _, _ in ins]
    arrays += dep
    in_specs += [pl.BlockSpec(memory_space=pl.ANY)] * len(dep)

    def body(*refs):
        kernel(*refs[: len(ins)], *refs[len(arrays) :])

    return pl.pallas_call(
        body,
        grid=grid,
        out_shape=shapes,
        in_specs=in_specs,
        out_specs=out_specs,
        compiler_params=params(),
        cost_estimate=cost(1000, nbytes),
    )(*arrays)


def vmem(arrays):
    return [(array, None, pltpu.VMEM) for array in arrays]


def over(n, step, body):
    step = min(n, step)

    def one(i, carry):
        body(pl.multiple_of(i * step, step), step)
        return carry

    lax.fori_loop(0, n // step, one, 0)


def cut(a, place, start, n, tile, dep):
    k, half = a.shape[1], a.shape[0] // 2

    def kernel(at, a_ref, *refs):
        refs[-1][...] = a_ref[...]

    return pl.pallas_call(
        kernel,
        grid_spec=pltpu.PrefetchScalarGridSpec(
            num_scalar_prefetch=1,
            grid=(n // tile,),
            in_specs=[pl.BlockSpec((tile, k), lambda i, at: ((1 - at[1]) * (half // tile) + start // tile + i, 0))]
            + [pl.BlockSpec(memory_space=pl.ANY)] * len(dep),
            out_specs=pl.BlockSpec((tile, k), lambda i, at: (i, 0)),
        ),
        out_shape=jax.ShapeDtypeStruct((n, k), BF16),
        compiler_params=params(),
        cost_estimate=cost(1000, 1000),
    )(place, a, *dep)


def order(place, pieces, dep):
    k = pieces[0].shape[1]

    def kernel(at, *refs):
        for d in range(4):
            to = (d + at[0]) % 4
            refs[4][pl.ds(pl.multiple_of(to * CHIP, CHIP), CHIP), :] = refs[d][...]

    ins = [(place, None, pltpu.SMEM)] + vmem(pieces)
    return run(kernel, (), [(((4 * CHIP, k), BF16), None, pltpu.VMEM)], ins, dep)[0]


def product(slabs, a, other, place, start, tile, dep):
    n, k = other.shape
    half = a.shape[0] // 2
    halves = len(slabs) // 2
    rows = slabs[0].shape[0]

    def kernel(at, *refs):
        s, (a_ref, o_ref), outs = refs[: 2 * halves], refs[2 * halves : 2 * halves + 2], refs[-halves:]
        for kind in range(halves):
            if halves == 1:
                mine, theirs = s[0][...], s[1][...]
            else:
                first = at[2] == kind
                mine, theirs = jnp.where(first, s[0][...], s[2][...]), jnp.where(first, s[1][...], s[3][...])
            total = dot(mine, a_ref[...]) + dot(theirs, o_ref[...])
            outs[kind][...] = total.astype(outs[kind].dtype)

    block = pl.BlockSpec((rows, tile), lambda i, at: (0, i))
    return pl.pallas_call(
        kernel,
        grid_spec=pltpu.PrefetchScalarGridSpec(
            num_scalar_prefetch=1,
            grid=(n // tile,),
            in_specs=[pl.BlockSpec((rows, k), lambda i, at: (0, 0))] * (2 * halves)
            + [
                pl.BlockSpec((tile, k), lambda i, at: (at[1] * (half // tile) + start // tile + i, 0)),
                pl.BlockSpec((tile, k), lambda i, at: (i, 0)),
            ]
            + [pl.BlockSpec(memory_space=pl.ANY)] * len(dep),
            out_specs=[block] * halves,
        ),
        out_shape=[jax.ShapeDtypeStruct((rows, n), dtype) for dtype in (F32, BF16)[:halves]],
        compiler_params=params(),
        cost_estimate=cost(1000, LONG),
    )(place, *slabs, a, other, *dep)


def added(refs, block, columns):
    total = None
    for ref in refs:
        term = wide(ref[block * CHIP : (block + 1) * CHIP, columns])
        total = term if total is None else total + term
    return total


class Unit:
    def __init__(self, terms, n):
        self.terms, self.n, self.half = terms, n, n // 2


def send(first, second, dep):
    n_first = first.half if first else 0
    n_second = second.half // 2 if second else 0
    ins = first.terms if first else []
    ins2 = second.terms + [second.up1, second.down1] if second else []

    def kernel(*refs):
        terms, terms2 = refs[: len(ins)], refs[len(ins) : len(ins) + len(ins2) - 2]
        up, down = refs[-2:]

        def one(c, step):
            left, right = pl.ds(c, step), pl.ds(n_first + c, step)
            up[:CHIP, left] = added(terms, 2, left).astype(BF16)
            up[CHIP:, left] = added(terms, 1, right).astype(BF16)
            down[:CHIP, left] = added(terms, 2, right).astype(BF16)
            down[CHIP:, left] = added(terms, 3, left).astype(BF16)

        def two(c, step):
            up1, down1 = refs[len(ins) + len(ins2) - 2 : len(ins) + len(ins2)]
            to = pl.ds(n_first + c, step)
            for i in range(2):
                rows = slice(i * CHIP, (i + 1) * CHIP)
                here = pl.ds(i * n_second + c, step)
                there = pl.ds((i + 2) * n_second + c, step)
                up[rows, to] = (added(terms2, 1, here) + wide(up1[:CHIP, here])).astype(BF16)
                down[rows, to] = (added(terms2, 3, there) + wide(down1[:CHIP, here])).astype(BF16)

        if first:
            over(n_first, 128, one)
        if second:
            over(n_second, 128, two)

    shape = (2 * CHIP, n_first + n_second), BF16
    up, down = run(kernel, (), [(shape, None, pltpu.VMEM)] * 2, vmem(ins + ins2), dep, LONG)
    up, down, dep = lax.ppermute(up, "gc", X_UP), lax.ppermute(down, "gc", X_DOWN), [down]
    if first:
        first.up1, first.down1 = up, down
    if second:
        second.up2, second.down2, second.at = up, down, n_first
    return dep


def sum_over_x(unit, outs, extra, store, dep):
    n_terms, half, at = len(unit.terms), unit.half, unit.at

    def kernel(*refs):
        terms = refs[:n_terms]
        up1, down1, up2, down2 = refs[n_terms : n_terms + 4]
        rest = refs[n_terms + 4 :]

        def one(c, step):
            for i in range(2):
                low, rows = i * (half // 2), slice(i * CHIP, (i + 1) * CHIP)
                here, moved = pl.ds(low + c, step), pl.ds(at + c, step)
                left = added(terms, 0, here) + wide(up2[rows, moved]) + wide(down1[CHIP:, here])
                store(low + c, step, left, rest)
                right = added(terms, 0, pl.ds(half + low + c, step)) + wide(down2[rows, moved]) + wide(up1[CHIP:, here])
                store(half + low + c, step, right, rest)

        over(half // 2, 128, one)

    ins = vmem(unit.terms + [unit.up1, unit.down1, unit.up2, unit.down2]) + extra
    return run(kernel, (), outs, ins, dep, LONG)


def keep(unit, dep):
    def store(c, step, total, refs):
        refs[0][:, pl.ds(c, step)] = total

    return sum_over_x(unit, [(((CHIP, unit.n), F32), None, pltpu.VMEM)], [], store, dep)[0]


def split_over_z(unit, held, place, dep):
    def store(c, step, total, refs):
        h, at, stays, goes = refs
        to = pl.ds(c, step)
        yes = at[2] == 0
        stays[:, to] = jnp.where(yes, h[:, to], total)
        goes[:, to] = jnp.where(yes, total, h[:, to]).astype(BF16)

    shape = CHIP, unit.n
    outs = [((shape, F32), None, pltpu.VMEM), ((shape, BF16), None, pltpu.VMEM)]
    return sum_over_x(unit, outs, vmem([held]) + [(place, None, pltpu.SMEM)], store, dep)


def split_rows(place, at, total):
    first = place[1] == 0
    top, low = total[:HALF], total[HALF:]
    return jnp.where(first, top, low), jnp.where(first, low, top)


def swap(stays, came, place, dep):
    n = stays.shape[1]

    def kernel(s, c, at, mine, theirs):
        def one(c0, step):
            to = pl.ds(c0, step)
            mine[:, to], theirs[:, to] = split_rows(at, None, s[:, to] + wide(c[:, to]))

        over(n, 128, one)

    shape = (HALF, n), F32
    return run(kernel, (), [(shape, None, pltpu.VMEM)] * 2, vmem([stays, came]) + [(place, None, pltpu.SMEM)], dep)


def keep_rows(unit, place, dep):
    def store(c, step, total, refs):
        at, mine, theirs = refs
        mine[:, pl.ds(c, step)], theirs[:, pl.ds(c, step)] = split_rows(at, None, total)

    outs = [(((HALF, unit.n), F32), None, pltpu.VMEM)] * 2
    return sum_over_x(unit, outs, [(place, None, pltpu.SMEM)], store, dep)


def wide(v):
    return v.astype(F32)


def shards(a, scaling):
    n_half = a.shape[0] // 2
    gr, at = lax.axis_index("gr"), lax.axis_index("gc")
    core, x, z_lo = at % 2, (at // 2) % 4, at // 8
    y, z_hi = gr % 4, gr // 4
    place = jnp.stack([(y - x + 4) % 4, core, z_lo ^ z_hi]).astype(jnp.int32)
    tile = n_half // 4
    start = [0]
    for size in UNITS:
        start.append(start[-1] + size * n_half // 1024)

    mine = (a[:SLAB_DEV].astype(F32) * scaling[None, :]).astype(BF16)
    y_up = lax.ppermute(mine, "gr", Y_UP)
    y_down = lax.ppermute(mine, "gr", Y_DOWN)
    y_far = lax.ppermute(mine, "gr", Y_FAR)
    z_far = lax.ppermute(mine, "gr", Z_FAR)
    near = [mine, y_down, y_far, y_up]
    far = [z_far, lax.ppermute(z_far, "gr", Y_DOWN), lax.ppermute(y_far, "gr", Z_FAR), lax.ppermute(z_far, "gr", Y_UP)]

    a = pltpu.with_memory_space_constraint(a, pltpu.HBM)
    dep = [y_up]
    others, parts = {}, {}

    slabs, units, held, z_parts, done = {}, {}, {}, {}, {}
    for what, *names in PLAN:
        name = names[0]
        if what == "cut":
            part = cut(a, place, start[name], start[name + 1] - start[name], tile, dep)
            parts[name] = part
            dep = [part]
        elif what == "order":
            dep = dep + [z_far]
            own = order(place, far if name else near, dep)
            slabs[name] = [own, lax.ppermute(own, "gc", CORE)]
            if name == 1:
                part = lax.optimization_barrier((parts[2], slabs[1][1]))[0]
                others[2] = lax.ppermute(part, "gc", CORE)
            if name == 0:
                for i in range(2):
                    last = parts[len(UNITS) - 1]
                    start_after = (y_down, y_far, z_far, last) if i == 0 else (slabs[0][1], others[i - 1])
                    part = lax.optimization_barrier((parts[i], *start_after))[0]
                    others[i] = lax.ppermute(part, "gc", CORE)
            dep = [own]
        elif what == "product":
            e, i = name
            operands = slabs[0] + slabs[1] if e == 2 else slabs[e]
            own, *sent = product(operands, a, others[i], place, start[i], tile, dep)
            units[name] = Unit([own] + [lax.ppermute(v, "gc", Z_NEAR) for v in sent], others[i].shape[0])
            dep = [own]
        elif what == "send":
            if name == (0, 1):
                dep = dep + far
            dep = send(*(units[name] if name else None for name in names), dep)
        elif what == "sum" and name[0] == 0:
            held[name[1]] = keep(units[name], dep)
            dep = [held[name[1]]]
        elif what == "sum" and name[0] == 1:
            stays, goes = split_over_z(units[name], held[name[1]], place, dep)
            z_parts[name[1]] = stays, lax.ppermute(goes, "gc", Z_NEAR)
            dep = [goes]
        else:
            if what == "swap":
                own, given = swap(*z_parts[name[1]], place, dep)
            else:
                own, given = keep_rows(units[name], place, dep)
            done[name[1]] = own, lax.ppermute(given, "gc", CORE)
            dep = [given]
    own, came = (jnp.concatenate([done[i][j] for i in range(len(UNITS))], axis=1) for j in range(2))
    first = core == 0
    return jnp.concatenate([jnp.where(first, own, came), jnp.where(first, came, own)], axis=1)


def solution(mesh):
    placed = (P("gr", "gc"), P("gc"))
    return jax.shard_map(shards, mesh=mesh, in_specs=placed, out_specs=P("gc", "gr"), check_vma=False)
```

```python
import jax
import jax.numpy as jnp
from jax import lax
from jax.experimental import pallas as pl
from jax.experimental.pallas import tpu as pltpu
from jax.sharding import PartitionSpec as P

F32, BF16 = jnp.float32, jnp.bfloat16
SLAB_DEV = 128
LONG = 100_000_000
HALF = 64
CHIP = 128
VMEM = 20 * 1024 * 1024

Y_UP = [(z * 4 + y, z * 4 + (y + 1) % 4) for z in range(2) for y in range(4)]
Y_DOWN = [(d, s) for s, d in Y_UP]
Y_FAR = [(z * 4 + y, z * 4 + (y + 2) % 4) for z in range(2) for y in range(4)]
Z_FAR = [(z * 4 + y, (1 - z) * 4 + y) for z in range(2) for y in range(4)]


def gc(z, x, c):
    return (z * 4 + x % 4) * 2 + c


EACH = [(z, x, c) for z in range(2) for x in range(4) for c in range(2)]
X_UP = [(gc(z, x, c), gc(z, x + 1, c)) for z, x, c in EACH]
X_DOWN = [(gc(z, x, c), gc(z, x - 1, c)) for z, x, c in EACH]
Z_NEAR = [(gc(z, x, c), gc(1 - z, x, c)) for z, x, c in EACH]
CORE = [(gc(z, x, c), gc(z, x, 1 - c)) for z, x, c in EACH]

UNITS = [256, 512, 256]
PLAN = [
    ("cut", 0),
    ("cut", 1),
    ("cut", 2),
    ("order", 0),
    ("product", (0, 0)),
    ("send", (0, 0), None),
    ("product", (0, 1)),
    ("send", (0, 1), (0, 0)),
    ("order", 1),
    ("product", (1, 1)),
    ("product", (2, 2)),
    ("send", (1, 1), (0, 1)),
    ("product", (1, 0)),
    ("sum", (0, 0)),
    ("send", (1, 0), (1, 1)),
    ("sum", (0, 1)),
    ("send", (2, 2), (1, 0)),
    ("sum", (1, 1)),
    ("sum", (1, 0)),
    ("send", None, (2, 2)),
    ("swap", (1, 1)),
    ("sum", (2, 2)),
    ("swap", (1, 0)),
]


def dot(s, a):
    return lax.dot_general(s, a, (((1,), (1,)), ((), ())), preferred_element_type=F32)


def cost(flops, nbytes):
    return pl.CostEstimate(flops=flops, bytes_accessed=nbytes, transcendentals=0)


def params():
    return pltpu.CompilerParams(vmem_limit_bytes=VMEM)


def run(kernel, grid, outs, ins, dep, nbytes=1000):
    shapes = [jax.ShapeDtypeStruct(shape, dtype) for (shape, dtype), _, _ in outs]
    spec = lambda block, where: pl.BlockSpec(block, where) if block else pl.BlockSpec(memory_space=where)
    out_specs = [spec(block, where) for _, block, where in outs]
    in_specs = [spec(block, where) for _, block, where in ins]
    arrays = [array for array, _, _ in ins]
    arrays += dep
    in_specs += [pl.BlockSpec(memory_space=pl.ANY)] * len(dep)

    def body(*refs):
        kernel(*refs[: len(ins)], *refs[len(arrays) :])

    return pl.pallas_call(
        body,
        grid=grid,
        out_shape=shapes,
        in_specs=in_specs,
        out_specs=out_specs,
        compiler_params=params(),
        cost_estimate=cost(1000, nbytes),
    )(*arrays)


def vmem(arrays):
    return [(array, None, pltpu.VMEM) for array in arrays]


def over(n, step, body):
    step = min(n, step)

    def one(i, carry):
        body(pl.multiple_of(i * step, step), step)
        return carry

    lax.fori_loop(0, n // step, one, 0)


def cut(a, place, start, n, tile, dep):
    k, half = a.shape[1], a.shape[0] // 2

    def kernel(at, a_ref, *refs):
        refs[-1][...] = a_ref[...]

    return pl.pallas_call(
        kernel,
        grid_spec=pltpu.PrefetchScalarGridSpec(
            num_scalar_prefetch=1,
            grid=(n // tile,),
            in_specs=[pl.BlockSpec((tile, k), lambda i, at: ((1 - at[1]) * (half // tile) + start // tile + i, 0))]
            + [pl.BlockSpec(memory_space=pl.ANY)] * len(dep),
            out_specs=pl.BlockSpec((tile, k), lambda i, at: (i, 0)),
        ),
        out_shape=jax.ShapeDtypeStruct((n, k), BF16),
        compiler_params=params(),
        cost_estimate=cost(1000, 1000),
    )(place, a, *dep)


def order(place, pieces, dep):
    k = pieces[0].shape[1]

    def kernel(at, *refs):
        for d in range(4):
            to = (d + at[0]) % 4
            refs[4][pl.ds(pl.multiple_of(to * CHIP, CHIP), CHIP), :] = refs[d][...]

    ins = [(place, None, pltpu.SMEM)] + vmem(pieces)
    return run(kernel, (), [(((4 * CHIP, k), BF16), None, pltpu.VMEM)], ins, dep)[0]


def product(slabs, a, other, place, start, tile, dep):
    n, k = other.shape
    half = a.shape[0] // 2
    halves = len(slabs) // 2
    rows = slabs[0].shape[0]

    def kernel(at, *refs):
        s, (a_ref, o_ref), outs = refs[: 2 * halves], refs[2 * halves : 2 * halves + 2], refs[-halves:]
        for kind in range(halves):
            if halves == 1:
                mine, theirs = s[0][...], s[1][...]
            else:
                first = at[2] == kind
                mine, theirs = jnp.where(first, s[0][...], s[2][...]), jnp.where(first, s[1][...], s[3][...])
            total = dot(mine, a_ref[...]) + dot(theirs, o_ref[...])
            outs[kind][...] = total.astype(outs[kind].dtype)

    block = pl.BlockSpec((rows, tile), lambda i, at: (0, i))
    return pl.pallas_call(
        kernel,
        grid_spec=pltpu.PrefetchScalarGridSpec(
            num_scalar_prefetch=1,
            grid=(n // tile,),
            in_specs=[pl.BlockSpec((rows, k), lambda i, at: (0, 0))] * (2 * halves)
            + [
                pl.BlockSpec((tile, k), lambda i, at: (at[1] * (half // tile) + start // tile + i, 0)),
                pl.BlockSpec((tile, k), lambda i, at: (i, 0)),
            ]
            + [pl.BlockSpec(memory_space=pl.ANY)] * len(dep),
            out_specs=[block] * halves,
        ),
        out_shape=[jax.ShapeDtypeStruct((rows, n), dtype) for dtype in (F32, BF16)[:halves]],
        compiler_params=params(),
        cost_estimate=cost(1000, LONG),
    )(place, *slabs, a, other, *dep)


def added(refs, block, columns):
    total = None
    for ref in refs:
        term = wide(ref[block * CHIP : (block + 1) * CHIP, columns])
        total = term if total is None else total + term
    return total


class Unit:
    def __init__(self, terms, n):
        self.terms, self.n, self.half = terms, n, n // 2


def send(first, second, dep):
    n_first = first.half if first else 0
    n_second = second.half // 2 if second else 0
    ins = first.terms if first else []
    ins2 = second.terms + [second.up1, second.down1] if second else []

    def kernel(*refs):
        terms, terms2 = refs[: len(ins)], refs[len(ins) : len(ins) + len(ins2) - 2]
        up, down = refs[-2:]

        def one(c, step):
            left, right = pl.ds(c, step), pl.ds(n_first + c, step)
            up[:CHIP, left] = added(terms, 2, left).astype(BF16)
            up[CHIP:, left] = added(terms, 1, right).astype(BF16)
            down[:CHIP, left] = added(terms, 2, right).astype(BF16)
            down[CHIP:, left] = added(terms, 3, left).astype(BF16)

        def two(c, step):
            up1, down1 = refs[len(ins) + len(ins2) - 2 : len(ins) + len(ins2)]
            to = pl.ds(n_first + c, step)
            for i in range(2):
                rows = slice(i * CHIP, (i + 1) * CHIP)
                here = pl.ds(i * n_second + c, step)
                there = pl.ds((i + 2) * n_second + c, step)
                up[rows, to] = (added(terms2, 1, here) + wide(up1[:CHIP, here])).astype(BF16)
                down[rows, to] = (added(terms2, 3, there) + wide(down1[:CHIP, here])).astype(BF16)

        if first:
            over(n_first, 256, one)
        if second:
            over(n_second, 256, two)

    shape = (2 * CHIP, n_first + n_second), BF16
    up, down = run(kernel, (), [(shape, None, pltpu.VMEM)] * 2, vmem(ins + ins2), dep, LONG)
    up, down, dep = lax.ppermute(up, "gc", X_UP), lax.ppermute(down, "gc", X_DOWN), [down]
    if first:
        first.up1, first.down1 = up, down
    if second:
        second.up2, second.down2, second.at = up, down, n_first
    return dep


def sum_over_x(unit, outs, extra, store, dep):
    n_terms, half, at = len(unit.terms), unit.half, unit.at

    def kernel(*refs):
        terms = refs[:n_terms]
        up1, down1, up2, down2 = refs[n_terms : n_terms + 4]
        rest = refs[n_terms + 4 :]

        def one(c, step):
            for i in range(2):
                low, rows = i * (half // 2), slice(i * CHIP, (i + 1) * CHIP)
                here, moved = pl.ds(low + c, step), pl.ds(at + c, step)
                left = added(terms, 0, here) + wide(up2[rows, moved]) + wide(down1[CHIP:, here])
                store(low + c, step, left, rest)
                right = added(terms, 0, pl.ds(half + low + c, step)) + wide(down2[rows, moved]) + wide(up1[CHIP:, here])
                store(half + low + c, step, right, rest)

        over(half // 2, 256, one)

    ins = vmem(unit.terms + [unit.up1, unit.down1, unit.up2, unit.down2]) + extra
    return run(kernel, (), outs, ins, dep, LONG)


def keep(unit, dep):
    def store(c, step, total, refs):
        refs[0][:, pl.ds(c, step)] = total

    return sum_over_x(unit, [(((CHIP, unit.n), F32), None, pltpu.VMEM)], [], store, dep)[0]


def split_over_z(unit, held, place, dep):
    def store(c, step, total, refs):
        h, at, stays, goes = refs
        to = pl.ds(c, step)
        yes = at[2] == 0
        stays[:, to] = jnp.where(yes, h[:, to], total)
        goes[:, to] = jnp.where(yes, total, h[:, to]).astype(BF16)

    shape = CHIP, unit.n
    outs = [((shape, F32), None, pltpu.VMEM), ((shape, BF16), None, pltpu.VMEM)]
    return sum_over_x(unit, outs, vmem([held]) + [(place, None, pltpu.SMEM)], store, dep)


def split_rows(place, at, total):
    first = place[1] == 0
    top, low = total[:HALF], total[HALF:]
    return jnp.where(first, top, low), jnp.where(first, low, top)


def swap(stays, came, place, dep):
    n = stays.shape[1]

    def kernel(s, c, at, mine, theirs):
        def one(c0, step):
            to = pl.ds(c0, step)
            mine[:, to], theirs[:, to] = split_rows(at, None, s[:, to] + wide(c[:, to]))

        over(n, 256, one)

    shape = (HALF, n), F32
    return run(kernel, (), [(shape, None, pltpu.VMEM)] * 2, vmem([stays, came]) + [(place, None, pltpu.SMEM)], dep)


def keep_rows(unit, place, dep):
    def store(c, step, total, refs):
        at, mine, theirs = refs
        mine[:, pl.ds(c, step)], theirs[:, pl.ds(c, step)] = split_rows(at, None, total)

    outs = [(((HALF, unit.n), F32), None, pltpu.VMEM)] * 2
    return sum_over_x(unit, outs, [(place, None, pltpu.SMEM)], store, dep)


def wide(v):
    return v.astype(F32)


def shards(a, scaling):
    n_half = a.shape[0] // 2
    gr, at = lax.axis_index("gr"), lax.axis_index("gc")
    core, x, z_lo = at % 2, (at // 2) % 4, at // 8
    y, z_hi = gr % 4, gr // 4
    place = jnp.stack([(y - x + 4) % 4, core, z_lo ^ z_hi]).astype(jnp.int32)
    tile = n_half // 4
    start = [0]
    for size in UNITS:
        start.append(start[-1] + size * n_half // 1024)

    mine = (a[:SLAB_DEV].astype(F32) * scaling[None, :]).astype(BF16)
    y_up = lax.ppermute(mine, "gr", Y_UP)
    y_down = lax.ppermute(mine, "gr", Y_DOWN)
    y_far = lax.ppermute(mine, "gr", Y_FAR)
    z_far = lax.ppermute(mine, "gr", Z_FAR)
    near = [mine, y_down, y_far, y_up]
    far = [z_far, lax.ppermute(z_far, "gr", Y_DOWN), lax.ppermute(y_far, "gr", Z_FAR), lax.ppermute(z_far, "gr", Y_UP)]

    a = pltpu.with_memory_space_constraint(a, pltpu.HBM)
    dep = [y_up]
    others, parts = {}, {}

    slabs, units, held, z_parts, done = {}, {}, {}, {}, {}
    for what, *names in PLAN:
        name = names[0]
        if what == "cut":
            part = cut(a, place, start[name], start[name + 1] - start[name], tile, dep)
            parts[name] = part
            dep = [part]
        elif what == "order":
            dep = dep + [z_far]
            own = order(place, far if name else near, dep)
            slabs[name] = [own, lax.ppermute(own, "gc", CORE)]
            if name == 0:
                for i in range(len(UNITS)):
                    start_after = (y_down, y_far, z_far) if i == 0 else (slabs[0][1], others[0])
                    part = lax.optimization_barrier((parts[i], *start_after))[0]
                    others[i] = lax.ppermute(part, "gc", CORE)
            dep = [own]
        elif what == "product":
            e, i = name
            if name == (0, 1):
                dep = dep + far
            operands = slabs[0] + slabs[1] if e == 2 else slabs[e]
            own, *sent = product(operands, a, others[i], place, start[i], tile, dep)
            units[name] = Unit([own] + [lax.ppermute(v, "gc", Z_NEAR) for v in sent], others[i].shape[0])
            dep = [own]
        elif what == "send":
            dep = send(*(units[name] if name else None for name in names), dep)
        elif what == "sum" and name[0] == 0:
            held[name[1]] = keep(units[name], dep)
            dep = [held[name[1]]]
        elif what == "sum" and name[0] == 1:
            stays, goes = split_over_z(units[name], held[name[1]], place, dep)
            z_parts[name[1]] = stays, lax.ppermute(goes, "gc", Z_NEAR)
            dep = [goes]
        else:
            if what == "swap":
                own, given = swap(*z_parts[name[1]], place, dep)
            else:
                own, given = keep_rows(units[name], place, dep)
            done[name[1]] = own, lax.ppermute(given, "gc", CORE)
            dep = [given]
    own, came = (jnp.concatenate([done[i][j] for i in range(len(UNITS))], axis=1) for j in range(2))
    first = core == 0
    return jnp.concatenate([jnp.where(first, own, came), jnp.where(first, came, own)], axis=1)


def solution(mesh):
    placed = (P("gr", "gc"), P("gc"))
    return jax.shard_map(shards, mesh=mesh, in_specs=placed, out_specs=P("gc", "gr"), check_vma=False)
```
